128 devices in a mesh: rows: 32 (over y_hi, x, z), cols: 4 (over y_lo, core).
Axes of the slice: x: 4, y: 4 (y_hi: 2, y_lo: 2; y = y_hi * 2 + y_lo), z: 4, core: 2. Of those that a mesh axis runs over, the one named last changes fastest.
Arguments:
- noise: bfloat16 [2, 2, 4096, 8192], P(None, None, 'rows', 'cols'), may hold values from -6 to 6
- root_eigen: bfloat16 [2, 4096, 8192], P(None, 'rows', 'cols'), may hold values from 0.19921875 to 2
Outputs:
- field: float32 [2, 8192, 8192], P(None, ('rows', 'cols'))
The draws below stay inside these ranges and needn't reach their ends.
All inputs are finite; a program needn't handle non-finite values.
Results may differ from the reference program's by a relative error of at most 0.0003.
Values sent between devices are 32-bit elements; how exact they have to be, the bound alone decides.
No kernel may reach another device: no remote copies, remote signals or barrier semaphores. Data moves between devices by JAX's collectives and lax.ppermute only.
A program may use at most 128 MiB of HBM per device.

```python
import math
import jax
import jax.numpy as jnp
from jax import lax

M = 8192
P_SIZE = 2
K = 4096


def block_levels(key, extent, cuts, least, top_value):
    factor_of, own = 1.0, jax.random.fold_in(key, 6)
    for axis_at, shards_of in cuts:
        heights = jnp.exp(jax.random.uniform(jax.random.fold_in(own, axis_at), (shards_of,), jnp.float32, least / len(cuts), top_value / len(cuts)))
        factor_of = factor_of * jnp.repeat(heights, extent[axis_at] // shards_of).reshape([-1 if axis == axis_at else 1 for axis in range(len(extent))])
    return factor_of


def bell_draw(rng, dims, spread, reach, pieces=(), dtype=jnp.bfloat16):
    loudness = block_levels(rng, dims, pieces, -0.22, 0.18) if pieces else 1.0
    values = jax.random.normal(rng, dims, jnp.float32) * spread * loudness
    return jnp.minimum(jnp.maximum(values, -reach), reach).astype(dtype)


def setup_inputs(seed: int = 0) -> dict:
    key_of = jax.random.split(jax.random.key(seed), 3)
    noise = bell_draw(key_of[0], (2, P_SIZE, K, M), 1.0, 6.0, ((2, 32), (3, 4)))
    root_eigen = jnp.clip(jnp.exp(math.log(2.0) - 2.306499 * jax.random.uniform(key_of[1], (P_SIZE, K, M), jnp.float32) ** block_levels(key_of[1], (P_SIZE, K, M), ((1, 32), (2, 4)), -0.2, 0.2)), 0.19921875, 2.0).astype(jnp.bfloat16)
    return dict(noise=noise, root_eigen=root_eigen)


def reference(noise, root_eigen):
    def plane_field(items):
        noise_plane, root_plane = items
        scale = root_plane.astype(jnp.float32)
        spectrum = scale * noise_plane[0].astype(jnp.float32) + 1j * (scale * noise_plane[1].astype(jnp.float32))
        columns = jnp.fft.ifft(spectrum, axis=1) * M
        mirror = jnp.conj(jnp.roll(jnp.flip(columns, 0), 1, axis=0))
        theta = 2.0 * jnp.pi * jnp.arange(K) / M
        twist = jnp.exp(1j * theta)[:, None]
        packed = (columns + mirror) + 1j * twist * (columns - mirror)
        planes = jnp.fft.ifft(packed, axis=0) * K
        joined = jnp.concatenate([planes.real, planes.imag], 0)
        return jnp.transpose(joined, (1, 0)) / M
    return lax.map(plane_field, (jnp.swapaxes(noise, 0, 1), root_eigen))
```

```python
import numpy as np
import jax
import jax.numpy as jnp
from jax import lax
from jax.experimental import pallas as pl
from jax.experimental.pallas import tpu as pltpu
from jax.sharding import PartitionSpec as P

VMEM_LIMIT = 48 * 1024 * 1024


def split_bf16(table):
    hi = jnp.asarray(table, jnp.float32).astype(jnp.bfloat16)
    lo = (jnp.asarray(table, jnp.float32) - hi.astype(jnp.float32)).astype(jnp.bfloat16)
    return hi, lo


def unit(num, den):
    ang = 2.0 * np.pi * (np.asarray(num) % den) / den
    return np.cos(ang), np.sin(ang)


def lane_tables():
    step = np.arange(128)
    cos, sin = unit(step[:, None] * step[None, :], 128)
    matrix = np.block([[cos, -sin], [sin, cos]])
    cos, sin = unit(np.arange(64)[:, None] * step[None, :], 8192)
    twist = np.stack([cos, sin], 1).reshape(128, 128)
    return matrix, twist.astype(np.float32)


def row_tables():
    src = np.arange(128)
    blocks = []
    for parity in (0, 1):
        cos, sin = unit(src[:, None] * (2 * np.arange(128) + parity)[None, :], 256)
        blocks.append(np.block([[cos, sin], [-sin, cos]]))
    matrix = np.concatenate(blocks, 1) / 4096.0
    twist = np.zeros((32, 8, 128))
    for parity in (0, 1):
        cos, sin = unit(np.arange(32)[:, None] * (2 * np.arange(128) + parity)[None, :], 8192)
        twist[:, 2 * parity] = cos
        twist[:, 2 * parity + 1] = sin
    return matrix, twist.astype(np.float32)


def cadd(a, b):
    return a[0] + b[0], a[1] + b[1]


def csub(a, b):
    return a[0] - b[0], a[1] - b[1]


def turn(a):
    return -a[1], a[0]


def cmul(a, cos, sin):
    return a[0] * cos - a[1] * sin, a[0] * sin + a[1] * cos


def dft4(v):
    s, d = cadd(v[0], v[2]), csub(v[0], v[2])
    t, u = cadd(v[1], v[3]), turn(csub(v[1], v[3]))
    return [cadd(s, t), cadd(d, u), csub(s, t), csub(d, u)]


HALF = float(np.sqrt(0.5))


def dft8(v):
    even, odd = dft4(v[0::2]), dft4(v[1::2])
    one = odd[1]
    one = ((one[0] - one[1]) * HALF, (one[0] + one[1]) * HALF)
    three = odd[3]
    three = ((-three[0] - three[1]) * HALF, (three[0] - three[1]) * HALF)
    odd = [odd[0], one, turn(odd[2]), three]
    return [cadd(even[i], odd[i]) for i in range(4)] + [csub(even[i], odd[i]) for i in range(4)]


def dft8_real(v):
    even, odd = dft4(v[0::2]), dft4(v[1::2])
    one, three = odd[1], odd[3]
    odd_re = [odd[0][0], (one[0] - one[1]) * HALF, -odd[2][1], (-three[0] - three[1]) * HALF]
    return [even[i][0] + odd_re[i] for i in range(4)] + [even[i][0] - odd_re[i] for i in range(4)]


def const_mul(a, num, den):
    num %= den
    if num == 0:
        return a
    if num * 4 == den:
        return turn(a)
    cos, sin = unit(num, den)
    return cmul(a, float(cos), float(sin))


def parts(x):
    hi = x.astype(jnp.bfloat16)
    return hi, (x - hi.astype(jnp.float32)).astype(jnp.bfloat16)


def spectrum_kernel(noise_ref, root_ref, out_ref):
    root = root_ref[0].astype(jnp.float32)
    out_ref[0, 0] = noise_ref[0, 0].astype(jnp.float32) * root
    out_ref[0, 1] = noise_ref[1, 0].astype(jnp.float32) * root


def spectrum(noise, root, plane):
    return pl.pallas_call(
        spectrum_kernel,
        grid=(4,),
        in_specs=[
            pl.BlockSpec((2, 1, 32, 2048), lambda i: (0, plane, i, 0)),
            pl.BlockSpec((1, 32, 2048), lambda i: (plane, i, 0)),
        ],
        out_specs=pl.BlockSpec((1, 2, 32, 2048), lambda i: (i, 0, 0, 0)),
        out_shape=jax.ShapeDtypeStruct((4, 2, 32, 2048), jnp.float32),
        compiler_params=pltpu.CompilerParams(vmem_limit_bytes=VMEM_LIMIT),
        cost_estimate=pl.CostEstimate(flops=1 << 20, bytes_accessed=7 << 19, transcendentals=0),
        name="spectrum",
    )(noise, root)


def columns_kernel(x_ref, hi_ref, lo_ref, twist_ref, out_ref, mid, turned):
    for low in range(8):
        v = []
        for high in range(8):
            block, col = high // 2, (high % 2) * 8 + low
            v.append(tuple(x_ref[block, s, :, col * 128:(col + 1) * 128] for s in (0, 1)))
        for b, value in enumerate(dft8(v)):
            value = const_mul(value, low * b, 64)
            for s in (0, 1):
                mid[s, b, low] = value[s]
    for b in range(8):
        v = [(mid[0, b, low], mid[1, b, low]) for low in range(8)]
        for h, value in enumerate(dft8(v)):
            y_low = b + 8 * h
            value = cmul(value, twist_ref[2 * y_low:2 * y_low + 1, :], twist_ref[2 * y_low + 1:2 * y_low + 2, :])
            for s in (0, 1):
                turned[s, pl.ds(y_low, 8, stride=64), :] = value[s]
    flat = out_ref.reshape(128 * 8, 128)
    dims = (((1,), (1,)), ((), ()))
    for half in range(2):
        rows = slice(half * 256, half * 256 + 256)
        hi, lo = parts(jnp.concatenate([turned[0, rows, :], turned[1, rows, :]], 1))
        result = lax.dot_general(hi_ref[...], hi, dims, preferred_element_type=jnp.float32)
        result += lax.dot_general(lo_ref[...], hi, dims, preferred_element_type=jnp.float32)
        result += lax.dot_general(hi_ref[...], lo, dims, preferred_element_type=jnp.float32)
        for pair in range(2):
            for s in (0, 1):
                flat[pl.ds((half * 2 + pair) * 2 + s, 128, stride=8), :] = result[
                    s * 128:(s + 1) * 128, pair * 128:(pair + 1) * 128
                ]


def columns(whole, hi, lo, twist):
    return pl.pallas_call(
        columns_kernel,
        grid=(4,),
        in_specs=[
            pl.BlockSpec((4, 2, 8, 2048), lambda i: (0, 0, i, 0)),
            pl.BlockSpec((256, 256), lambda i: (0, 0)),
            pl.BlockSpec((256, 256), lambda i: (0, 0)),
            pl.BlockSpec((128, 128), lambda i: (0, 0)),
        ],
        out_specs=pl.BlockSpec((128, 8, 128), lambda i: (0, i, 0)),
        out_shape=jax.ShapeDtypeStruct((128, 32, 128), jnp.float32),
        scratch_shapes=[
            pltpu.VMEM((2, 8, 8, 8, 128), jnp.float32),
            pltpu.VMEM((2, 512, 128), jnp.float32),
        ],
        compiler_params=pltpu.CompilerParams(vmem_limit_bytes=VMEM_LIMIT),
        cost_estimate=pl.CostEstimate(flops=3 << 28, bytes_accessed=4 << 20, transcendentals=0),
        name="columns",
    )(whole, hi, lo, twist)


def rows_kernel(c_ref, hi_ref, lo_ref, twist_ref, *rest):
    out_ref, steps = rest[-2:]
    flat = c_ref.reshape(128 * 32, 128)

    def one_pair(pair, _):
        re = flat[pl.ds(2 * pair, 128, stride=32), :]
        im = flat[pl.ds(2 * pair + 1, 128, stride=32), :]
        both = jnp.concatenate([re.T, im.T], 1)
        hi, lo = parts(both)
        result = jnp.dot(hi, hi_ref[...], preferred_element_type=jnp.float32)
        result += jnp.dot(hi, lo_ref[...], preferred_element_type=jnp.float32)
        result += jnp.dot(lo, hi_ref[...], preferred_element_type=jnp.float32)
        for k in (0, 1):
            rows = slice(64 * k, 64 * k + 64)
            for parity in (0, 1):
                at = parity * 256
                value = (result[rows, at:at + 128], result[rows, at + 128:at + 256])
                value = cmul(
                    value,
                    twist_ref[2 * pair + k, 2 * parity:2 * parity + 1, :],
                    twist_ref[2 * pair + k, 2 * parity + 1:2 * parity + 2, :],
                )
                for s in (0, 1):
                    steps[2 * parity + s, 2 * pair + k] = value[s]
        @pl.when(pair == 0)
        def _():
            steps[0, 0] -= im.T[0:64, 0:1] * (1.0 / 4096.0)
            steps[2, 0] -= re.T[0:64, 0:1] * (1.0 / 4096.0)
        return 0

    lax.fori_loop(0, 16, one_pair, 0)

    def one_group(group, _):
        at = pl.multiple_of(group * 8, 8)
        for parity in (0, 1):
            mid = [[None] * 8 for _ in range(4)]
            for low in range(8):
                v = [tuple(steps[2 * parity + s, 8 * high + low, pl.ds(at, 8), :] for s in (0, 1)) for high in range(4)]
                for b, value in enumerate(dft4(v)):
                    mid[b][low] = const_mul(value, low * b, 32)
            for b in range(4):
                for h, value in enumerate(dft8_real(mid[b])):
                    col = (parity * 32 + b + 4 * h) * 128
                    out_ref[0, pl.ds(at, 8), col:col + 128] = value
        return 0

    lax.fori_loop(0, 8, one_group, 0)


def rows(full, hi, lo, twist, plane, field=None):
    whole = lambda *dims: pl.BlockSpec(dims, lambda i: (0,) * len(dims))
    operands = [full, hi, lo, twist]
    specs = [whole(128, 32, 128), whole(256, 512), whole(256, 512), whole(32, 8, 128)]
    if field is not None:
        operands.append(field)
        specs.append(pl.BlockSpec(memory_space=pl.ANY))
    return pl.pallas_call(
        rows_kernel,
        grid=(1,),
        in_specs=specs,
        out_specs=pl.BlockSpec((1, 64, 8192), lambda i: (plane, 0, 0)),
        out_shape=jax.ShapeDtypeStruct((2, 64, 8192), jnp.float32),
        scratch_shapes=[pltpu.VMEM((4, 32, 64, 128), jnp.float32)],
        input_output_aliases={} if field is None else {4: 0},
        compiler_params=pltpu.CompilerParams(vmem_limit_bytes=VMEM_LIMIT),
        cost_estimate=pl.CostEstimate(flops=3 << 29, bytes_accessed=4 << 20, transcendentals=0),
        name="rows",
    )(*operands)


def shards(noise, root):
    lane_matrix, lane_twist = lane_tables()
    row_matrix, row_twist = row_tables()
    lane_hi, lane_lo = split_bf16(lane_matrix)
    row_hi, row_lo = split_bf16(row_matrix)
    field = None
    full = []
    for plane in range(2):
        sent = spectrum(noise, root, plane)
        whole = lax.all_to_all(sent, "cols", 0, 0, tiled=True)
        blocks = columns(whole, lane_hi, lane_lo, jnp.asarray(lane_twist))
        full.append(lax.all_to_all(blocks, ("rows", "cols"), 0, 0, tiled=True))
    for plane in range(2):
        field = rows(full[plane], row_hi, row_lo, jnp.asarray(row_twist), plane, field)
    return field


def solution(mesh):
    return jax.shard_map(
        shards,
        mesh=mesh,
        in_specs=(P(None, None, "rows", "cols"), P(None, "rows", "cols")),
        out_specs=P(None, ("rows", "cols"), None),
        check_vma=False,
    )
```

```python
import numpy as np
import jax
import jax.numpy as jnp
from jax import lax
from jax.experimental import pallas as pl
from jax.experimental.pallas import tpu as pltpu
from jax.sharding import PartitionSpec as P

VMEM_LIMIT = 48 * 1024 * 1024


def split_bf16(table):
    hi = jnp.asarray(table, jnp.float32).astype(jnp.bfloat16)
    lo = (jnp.asarray(table, jnp.float32) - hi.astype(jnp.float32)).astype(jnp.bfloat16)
    return hi, lo


def unit(num, den):
    ang = 2.0 * np.pi * (np.asarray(num) % den) / den
    return np.cos(ang), np.sin(ang)


def lane_tables():
    step = np.arange(128)
    cos, sin = unit(step[:, None] * step[None, :], 128)
    matrix = np.block([[cos, -sin], [sin, cos]])
    cos, sin = unit(np.arange(64)[:, None] * step[None, :], 8192)
    twist = np.stack([cos, sin], 1).reshape(128, 128)
    return matrix, twist.astype(np.float32)


def row_tables():
    src = np.arange(128)
    blocks = []
    for parity in (0, 1):
        cos, sin = unit(src[:, None] * (2 * np.arange(128) + parity)[None, :], 256)
        blocks.append(np.block([[cos, sin], [-sin, cos]]))
    matrix = np.concatenate(blocks, 1) / 4096.0
    twist = np.zeros((32, 8, 128))
    for parity in (0, 1):
        cos, sin = unit(np.arange(32)[:, None] * (2 * np.arange(128) + parity)[None, :], 8192)
        twist[:, 2 * parity] = cos
        twist[:, 2 * parity + 1] = sin
    return matrix, twist.astype(np.float32)


def cadd(a, b):
    return a[0] + b[0], a[1] + b[1]


def csub(a, b):
    return a[0] - b[0], a[1] - b[1]


def turn(a):
    return -a[1], a[0]


def cmul(a, cos, sin):
    return a[0] * cos - a[1] * sin, a[0] * sin + a[1] * cos


def dft4(v):
    s, d = cadd(v[0], v[2]), csub(v[0], v[2])
    t, u = cadd(v[1], v[3]), turn(csub(v[1], v[3]))
    return [cadd(s, t), cadd(d, u), csub(s, t), csub(d, u)]


HALF = float(np.sqrt(0.5))


def dft8(v):
    even, odd = dft4(v[0::2]), dft4(v[1::2])
    one = odd[1]
    one = ((one[0] - one[1]) * HALF, (one[0] + one[1]) * HALF)
    three = odd[3]
    three = ((-three[0] - three[1]) * HALF, (three[0] - three[1]) * HALF)
    odd = [odd[0], one, turn(odd[2]), three]
    return [cadd(even[i], odd[i]) for i in range(4)] + [csub(even[i], odd[i]) for i in range(4)]


def dft8_real(v):
    even, odd = dft4(v[0::2]), dft4(v[1::2])
    one, three = odd[1], odd[3]
    odd_re = [odd[0][0], (one[0] - one[1]) * HALF, -odd[2][1], (-three[0] - three[1]) * HALF]
    return [even[i][0] + odd_re[i] for i in range(4)] + [even[i][0] - odd_re[i] for i in range(4)]


def const_mul(a, num, den):
    num %= den
    if num == 0:
        return a
    if num * 4 == den:
        return turn(a)
    cos, sin = unit(num, den)
    return cmul(a, float(cos), float(sin))


def parts(x):
    hi = x.astype(jnp.bfloat16)
    return hi, (x - hi.astype(jnp.float32)).astype(jnp.bfloat16)


def spectrum_kernel(col_ref, noise_ref, root_ref, *outs):
    for plane in range(2):
        for d in range(4):
            rows = pl.ds(pl.multiple_of((col_ref[0] ^ d) * 32, 32), 32)
            root = root_ref[plane, rows, :].astype(jnp.float32)
            for s in (0, 1):
                outs[4 * plane + d][s] = noise_ref[s, plane, rows, :].astype(jnp.float32) * root


def spectrum(col, noise, root):
    return pl.pallas_call(
        spectrum_kernel,
        grid_spec=pltpu.PrefetchScalarGridSpec(
            num_scalar_prefetch=1,
            grid=(1,),
            in_specs=[
                pl.BlockSpec((2, 2, 128, 2048), lambda i, c: (0, 0, 0, 0)),
                pl.BlockSpec((2, 128, 2048), lambda i, c: (0, 0, 0)),
            ],
            out_specs=[pl.BlockSpec((2, 32, 2048), lambda i, c: (0, 0, 0))] * 8,
        ),
        out_shape=[jax.ShapeDtypeStruct((2, 32, 2048), jnp.float32)] * 8,
        compiler_params=pltpu.CompilerParams(vmem_limit_bytes=VMEM_LIMIT),
        cost_estimate=pl.CostEstimate(flops=1 << 21, bytes_accessed=7 << 20, transcendentals=0),
        name="spectrum",
    )(col, noise, root)


def by_index(values, index):
    odd, upper = (index & 1) == 1, (index & 2) == 2
    pick = lambda flag, a, b: tuple(jnp.where(flag, p, q) for p, q in zip(a, b))
    v = [pick(odd, values[d ^ 1], values[d]) for d in range(4)]
    return [pick(upper, v[d ^ 2], v[d]) for d in range(4)]


def columns_kernel(col_ref, x0, x1, x2, x3, hi_ref, lo_ref, twist_ref, out_ref, mid, turned):
    for low in range(8):
        v = [None] * 8
        for half in range(2):
            at = (half * 8 + low) * 128
            got = [tuple(x[s, :, at:at + 128] for s in (0, 1)) for x in (x0, x1, x2, x3)]
            v[half::2] = by_index(got, col_ref[0])
        for b, value in enumerate(dft8(v)):
            value = const_mul(value, low * b, 64)
            for s in (0, 1):
                mid[s, b, low] = value[s]
    for b in range(8):
        v = [(mid[0, b, low], mid[1, b, low]) for low in range(8)]
        for h, value in enumerate(dft8(v)):
            y_low = b + 8 * h
            value = cmul(value, twist_ref[2 * y_low:2 * y_low + 1, :], twist_ref[2 * y_low + 1:2 * y_low + 2, :])
            for s in (0, 1):
                turned[s, pl.ds(y_low, 8, stride=64), :] = value[s]
    flat = out_ref.reshape(128 * 8, 128)
    dims = (((1,), (1,)), ((), ()))
    for half in range(2):
        rows = slice(half * 256, half * 256 + 256)
        hi, lo = parts(jnp.concatenate([turned[0, rows, :], turned[1, rows, :]], 1))
        result = lax.dot_general(hi_ref[...], hi, dims, preferred_element_type=jnp.float32)
        result += lax.dot_general(lo_ref[...], hi, dims, preferred_element_type=jnp.float32)
        result += lax.dot_general(hi_ref[...], lo, dims, preferred_element_type=jnp.float32)
        for pair in range(2):
            for s in (0, 1):
                flat[pl.ds((half * 2 + pair) * 2 + s, 128, stride=8), :] = result[
                    s * 128:(s + 1) * 128, pair * 128:(pair + 1) * 128
                ]


def columns(col, pieces, hi, lo, twist, flops):
    return pl.pallas_call(
        columns_kernel,
        grid_spec=pltpu.PrefetchScalarGridSpec(
            num_scalar_prefetch=1,
            grid=(4,),
            in_specs=[pl.BlockSpec((2, 8, 2048), lambda i, c: (0, i, 0))] * 4
            + [
                pl.BlockSpec((256, 256), lambda i, c: (0, 0)),
                pl.BlockSpec((256, 256), lambda i, c: (0, 0)),
                pl.BlockSpec((128, 128), lambda i, c: (0, 0)),
            ],
            out_specs=pl.BlockSpec((128, 8, 128), lambda i, c: (0, i, 0)),
            scratch_shapes=[
                pltpu.VMEM((2, 8, 8, 8, 128), jnp.float32),
                pltpu.VMEM((2, 512, 128), jnp.float32),
            ],
        ),
        out_shape=jax.ShapeDtypeStruct((128, 32, 128), jnp.float32),
        compiler_params=pltpu.CompilerParams(vmem_limit_bytes=VMEM_LIMIT),
        cost_estimate=pl.CostEstimate(flops=flops, bytes_accessed=4 << 20, transcendentals=0),
        name="columns",
    )(col, *pieces, hi, lo, twist)


def rows_kernel(c_ref, hi_ref, lo_ref, twist_ref, *rest):
    out_ref, steps = rest[-2:]
    flat = c_ref.reshape(128 * 32, 128)

    def one_pair(pair, _):
        re = flat[pl.ds(2 * pair, 128, stride=32), :]
        im = flat[pl.ds(2 * pair + 1, 128, stride=32), :]
        both = jnp.concatenate([re.T, im.T], 1)
        hi, lo = parts(both)
        result = jnp.dot(hi, hi_ref[...], preferred_element_type=jnp.float32)
        result += jnp.dot(hi, lo_ref[...], preferred_element_type=jnp.float32)
        result += jnp.dot(lo, hi_ref[...], preferred_element_type=jnp.float32)
        for k in (0, 1):
            rows = slice(64 * k, 64 * k + 64)
            for parity in (0, 1):
                at = parity * 256
                value = (result[rows, at:at + 128], result[rows, at + 128:at + 256])
                value = cmul(
                    value,
                    twist_ref[2 * pair + k, 2 * parity:2 * parity + 1, :],
                    twist_ref[2 * pair + k, 2 * parity + 1:2 * parity + 2, :],
                )
                for s in (0, 1):
                    steps[2 * parity + s, 2 * pair + k] = value[s]
        @pl.when(pair == 0)
        def _():
            steps[0, 0] -= im.T[0:64, 0:1] * (1.0 / 4096.0)
            steps[2, 0] -= re.T[0:64, 0:1] * (1.0 / 4096.0)
        return 0

    lax.fori_loop(0, 16, one_pair, 0)

    def one_group(group, _):
        at = pl.multiple_of(group * 8, 8)
        for parity in (0, 1):
            mid = [[None] * 8 for _ in range(4)]
            for low in range(8):
                v = [tuple(steps[2 * parity + s, 8 * high + low, pl.ds(at, 8), :] for s in (0, 1)) for high in range(4)]
                for b, value in enumerate(dft4(v)):
                    mid[b][low] = const_mul(value, low * b, 32)
            for b in range(4):
                for h, value in enumerate(dft8_real(mid[b])):
                    col = (parity * 32 + b + 4 * h) * 128
                    out_ref[0, pl.ds(at, 8), col:col + 128] = value
        return 0

    lax.fori_loop(0, 8, one_group, 0)


def rows(full, hi, lo, twist, plane, field=None):
    whole = lambda *dims: pl.BlockSpec(dims, lambda i: (0,) * len(dims))
    operands = [full, hi, lo, twist]
    specs = [whole(128, 32, 128), whole(256, 512), whole(256, 512), whole(32, 8, 128)]
    if field is not None:
        operands.append(field)
        specs.append(pl.BlockSpec(memory_space=pl.ANY))
    return pl.pallas_call(
        rows_kernel,
        grid=(1,),
        in_specs=specs,
        out_specs=pl.BlockSpec((1, 64, 8192), lambda i: (plane, 0, 0)),
        out_shape=jax.ShapeDtypeStruct((2, 64, 8192), jnp.float32),
        scratch_shapes=[pltpu.VMEM((4, 32, 64, 128), jnp.float32)],
        input_output_aliases={} if field is None else {4: 0},
        compiler_params=pltpu.CompilerParams(vmem_limit_bytes=VMEM_LIMIT),
        cost_estimate=pl.CostEstimate(flops=3 << 29, bytes_accessed=4 << 20, transcendentals=0),
        name="rows",
    )(*operands)


def shards(noise, root):
    lane_matrix, lane_twist = lane_tables()
    row_matrix, row_twist = row_tables()
    lane_hi, lane_lo = split_bf16(lane_matrix)
    row_hi, row_lo = split_bf16(row_matrix)
    col = lax.axis_index("cols")[None]
    field = None
    full = []
    sent = spectrum(col, noise, root)
    got = [sent[0:4], sent[4:8]]
    for plane in range(2):
        got[plane] = list(got[plane])
        for d in (2, 3, 1):
            got[plane][d] = lax.ppermute(got[plane][d], "cols", [(c, c ^ d) for c in range(4)])
    for plane in range(2):
        pieces = got[plane]
        blocks = columns(col, pieces, lane_hi, lane_lo, jnp.asarray(lane_twist), 3 << (28 + 8 * plane))
        full.append(lax.all_to_all(blocks, ("rows", "cols"), 0, 0, tiled=True))
    for plane in range(2):
        field = rows(full[plane], row_hi, row_lo, jnp.asarray(row_twist), plane, field)
    return field


def solution(mesh):
    return jax.shard_map(
        shards,
        mesh=mesh,
        in_specs=(P(None, None, "rows", "cols"), P(None, "rows", "cols")),
        out_specs=P(None, ("rows", "cols"), None),
        check_vma=False,
    )
```

```python
import functools

import numpy as np
import jax
import jax.numpy as jnp
from jax import lax
from jax.experimental import pallas as pl
from jax.experimental.pallas import tpu as pltpu
from jax.sharding import Mesh, PartitionSpec as P

PITCH = 72
VMEM_LIMIT = 48 * 1024 * 1024


def split_bf16(table):
    hi = jnp.asarray(table, jnp.float32).astype(jnp.bfloat16)
    lo = (jnp.asarray(table, jnp.float32) - hi.astype(jnp.float32)).astype(jnp.bfloat16)
    return hi, lo


def unit(num, den):
    ang = 2.0 * np.pi * (np.asarray(num) % den) / den
    return np.cos(ang), np.sin(ang)


ROWS, COLS = ("y_hi", "x", "z"), ("y_lo", "core")
ORDER_AXES = ("core", "z", "y_hi", "y_lo", "x")
ORDER = np.arange(128).reshape(2, 4, 4, 2, 2).transpose(4, 2, 0, 3, 1).reshape(128)


def lane_tables():
    step = np.arange(128)
    cos, sin = unit(ORDER[:, None] * step[None, :], 128)
    matrix = np.block([[cos, -sin], [sin, cos]])
    cos, sin = unit(np.arange(64)[:, None] * step[None, :], 8192)
    twist = np.stack([cos, sin], 1).reshape(128, 128)
    return matrix, twist.astype(np.float32)


def row_tables():
    src = ORDER
    blocks = []
    for parity in (0, 1):
        cos, sin = unit(src[:, None] * (2 * np.arange(128) + parity)[None, :], 256)
        blocks.append(np.block([[cos, sin], [-sin, cos]]))
    matrix = np.concatenate(blocks, 1) / 4096.0
    twist = np.zeros((32, 8, 128))
    for parity in (0, 1):
        cos, sin = unit(np.arange(32)[:, None] * (2 * np.arange(128) + parity)[None, :], 8192)
        twist[:, 2 * parity] = cos
        twist[:, 2 * parity + 1] = sin
    return matrix, twist.astype(np.float32)


def cadd(a, b):
    return a[0] + b[0], a[1] + b[1]


def csub(a, b):
    return a[0] - b[0], a[1] - b[1]


def turn(a):
    return -a[1], a[0]


def cmul(a, cos, sin):
    return a[0] * cos - a[1] * sin, a[0] * sin + a[1] * cos


def dft4(v):
    s, d = cadd(v[0], v[2]), csub(v[0], v[2])
    t, u = cadd(v[1], v[3]), turn(csub(v[1], v[3]))
    return [cadd(s, t), cadd(d, u), csub(s, t), csub(d, u)]


HALF = float(np.sqrt(0.5))


def dft8(v):
    even, odd = dft4(v[0::2]), dft4(v[1::2])
    one = odd[1]
    one = ((one[0] - one[1]) * HALF, (one[0] + one[1]) * HALF)
    three = odd[3]
    three = ((-three[0] - three[1]) * HALF, (three[0] - three[1]) * HALF)
    odd = [odd[0], one, turn(odd[2]), three]
    return [cadd(even[i], odd[i]) for i in range(4)] + [csub(even[i], odd[i]) for i in range(4)]


def dft8_real(v):
    even, odd = dft4(v[0::2]), dft4(v[1::2])
    one, three = odd[1], odd[3]
    odd_re = [odd[0][0], (one[0] - one[1]) * HALF, -odd[2][1], (-three[0] - three[1]) * HALF]
    return [even[i][0] + odd_re[i] for i in range(4)] + [even[i][0] - odd_re[i] for i in range(4)]


def const_mul(a, num, den):
    num %= den
    if num == 0:
        return a
    if num * 4 == den:
        return turn(a)
    cos, sin = unit(num, den)
    return cmul(a, float(cos), float(sin))


def parts(x):
    hi = x.astype(jnp.bfloat16)
    return hi, (x - hi.astype(jnp.float32)).astype(jnp.bfloat16)


def spectrum_kernel(plane, partners, col_ref, noise_ref, root_ref, *rest):
    outs, (noise, root, arrived) = rest[:len(partners)], rest[len(partners):]
    copies = []
    for i, d in enumerate(partners):
        rows = pl.ds(pl.multiple_of((col_ref[0] ^ d) * 32, 32), 32)
        copies.append([
            pltpu.make_async_copy(noise_ref.at[0, plane, rows], noise.at[i, 0], arrived.at[i, 0]),
            pltpu.make_async_copy(noise_ref.at[1, plane, rows], noise.at[i, 1], arrived.at[i, 1]),
            pltpu.make_async_copy(root_ref.at[plane, rows], root.at[i], arrived.at[i, 2]),
        ])
        for copy in copies[-1]:
            copy.start()
    for i, out in enumerate(outs):
        for copy in copies[i]:
            copy.wait()
        scale = root[i].astype(jnp.float32)
        for s in (0, 1):
            out[s] = noise[i, s].astype(jnp.float32) * scale


def spectrum(col, noise, root, plane, partners, limit):
    n = len(partners)
    return pl.pallas_call(
        functools.partial(spectrum_kernel, plane, partners),
        grid_spec=pltpu.PrefetchScalarGridSpec(
            num_scalar_prefetch=1,
            grid=(1,),
            in_specs=[pl.BlockSpec(memory_space=pltpu.HBM)] * 2,
            out_specs=[pl.BlockSpec((2, 32, 2048), lambda i, c: (0, 0, 0))] * n,
            scratch_shapes=[
                pltpu.VMEM((n, 2, 32, 2048), jnp.bfloat16),
                pltpu.VMEM((n, 32, 2048), jnp.bfloat16),
                pltpu.SemaphoreType.DMA((n, 3)),
            ],
        ),
        out_shape=[jax.ShapeDtypeStruct((2, 32, 2048), jnp.float32)] * n,
        compiler_params=pltpu.CompilerParams(vmem_limit_bytes=limit),
        cost_estimate=pl.CostEstimate(flops=n << 18, bytes_accessed=n * (7 << 17), transcendentals=0),
        name="spectrum",
    )(col, noise, root)


def by_index(values, index):
    odd, upper = (index & 1) == 1, (index & 2) == 2
    pick = lambda flag, a, b: tuple(jnp.where(flag, p, q) for p, q in zip(a, b))
    v = [pick(odd, values[d ^ 1], values[d]) for d in range(4)]
    return [pick(upper, v[d ^ 2], v[d]) for d in range(4)]


def columns_kernel(col_ref, x0, x1, x2, x3, hi_ref, lo_ref, twist_ref, out_ref, mid, turned):
    for low in range(8):
        v = [None] * 8
        for half in range(2):
            at = (half * 8 + low) * 128
            got = [tuple(x[s, :, at:at + 128] for s in (0, 1)) for x in (x0, x1, x2, x3)]
            v[half::2] = by_index(got, col_ref[0])
        for b, value in enumerate(dft8(v)):
            value = const_mul(value, low * b, 64)
            for s in (0, 1):
                mid[s, b, low] = value[s]
    for b in range(8):
        v = [(mid[0, b, low], mid[1, b, low]) for low in range(8)]
        for h, value in enumerate(dft8(v)):
            y_low = b + 8 * h
            value = cmul(value, twist_ref[2 * y_low:2 * y_low + 1, :], twist_ref[2 * y_low + 1:2 * y_low + 2, :])
            for s in (0, 1):
                turned[s, pl.ds(y_low, 8, stride=PITCH), :] = value[s]
    flat = out_ref.reshape(128 * 8, 128)
    dims = (((1,), (1,)), ((), ()))
    for half in range(2):
        rows = [slice(k * PITCH, k * PITCH + 64) for k in range(4 * half, 4 * half + 4)]
        hi, lo = parts(jnp.concatenate([jnp.concatenate([turned[s, r, :] for r in rows], 0) for s in (0, 1)], 1))
        result = lax.dot_general(hi_ref[...], hi, dims, preferred_element_type=jnp.float32)
        result += lax.dot_general(lo_ref[...], hi, dims, preferred_element_type=jnp.float32)
        result += lax.dot_general(hi_ref[...], lo, dims, preferred_element_type=jnp.float32)
        for pair in range(2):
            for s in (0, 1):
                flat[pl.ds((half * 2 + pair) * 2 + s, 128, stride=8), :] = result[
                    s * 128:(s + 1) * 128, pair * 128:(pair + 1) * 128
                ]


def columns(col, pieces, hi, lo, twist, flops):
    return pl.pallas_call(
        columns_kernel,
        grid_spec=pltpu.PrefetchScalarGridSpec(
            num_scalar_prefetch=1,
            grid=(4,),
            in_specs=[pl.BlockSpec((2, 8, 2048), lambda i, c: (0, i, 0))] * 4
            + [
                pl.BlockSpec((256, 256), lambda i, c: (0, 0)),
                pl.BlockSpec((256, 256), lambda i, c: (0, 0)),
                pl.BlockSpec((128, 128), lambda i, c: (0, 0)),
            ],
            out_specs=pl.BlockSpec((128, 8, 128), lambda i, c: (0, i, 0)),
            scratch_shapes=[
                pltpu.VMEM((2, 8, 8, 8, 128), jnp.float32),
                pltpu.VMEM((2, 8 * PITCH, 128), jnp.float32),
            ],
        ),
        out_shape=jax.ShapeDtypeStruct((128, 32, 128), jnp.float32),
        compiler_params=pltpu.CompilerParams(vmem_limit_bytes=VMEM_LIMIT),
        cost_estimate=pl.CostEstimate(flops=flops, bytes_accessed=4 << 20, transcendentals=0),
        name="columns",
    )(col, *pieces, hi, lo, twist)


def rows_kernel(plane, c_ref, hi_ref, lo_ref, twist_ref, *rest):
    out_ref, steps, ready, sent = rest[-4:]
    flat = c_ref.reshape(128 * 32, 128)

    def some_pairs(step, _):
        both = []
        for t in range(8):
            at = 2 * (8 * step + t)
            both.append(jnp.concatenate([flat[pl.ds(at + s, 128, stride=32), :].T for s in (0, 1)], 1))
        hi, lo = parts(jnp.concatenate(both, 0))
        result = jnp.dot(hi, hi_ref[...], preferred_element_type=jnp.float32)
        result += jnp.dot(hi, lo_ref[...], preferred_element_type=jnp.float32)
        result += jnp.dot(lo, hi_ref[...], preferred_element_type=jnp.float32)
        for t in range(16):
            k = 16 * step + t
            for parity in (0, 1):
                re, im = (result[64 * t:64 * t + 64, at:at + 128] for at in (256 * parity, 256 * parity + 128))
                twist = (twist_ref[k, j:j + 1, :] for j in (2 * parity, 2 * parity + 1))
                for s, value in enumerate(cmul((re, im), *twist)):
                    steps[2 * parity + s, k] = value
        return 0

    lax.fori_loop(0, 2, some_pairs, 0)
    for s in (0, 1):
        first = flat[pl.ds(s, 128, stride=32), :].T[0:64, 0:1] * (1.0 / 4096.0)
        steps[2 - 2 * s, 0] -= first

    def copy(group):
        part = pl.ds(pl.multiple_of(group * 8, 8), 8)
        return pltpu.make_async_copy(ready.at[part], out_ref.at[plane, part], sent.at[group])

    def one_group(group, _):
        here = pl.ds(pl.multiple_of(group * 8, 8), 8)
        for parity in (0, 1):
            mid = [[None] * 8 for _ in range(4)]
            for low in range(8):
                v = [tuple(steps[2 * parity + s, 8 * high + low, here, :] for s in (0, 1)) for high in range(4)]
                for b, value in enumerate(dft4(v)):
                    mid[b][low] = const_mul(value, low * b, 32)
            for b in range(4):
                for h, value in enumerate(dft8_real(mid[b])):
                    col = (parity * 32 + b + 4 * h) * 128
                    ready[here, col:col + 128] = value
        copy(group).start()
        return 0

    lax.fori_loop(0, 8, one_group, 0, unroll=True)
    for group in range(8):
        copy(group).wait()


def rows(full, hi, lo, twist, plane, field=None):
    whole = lambda *dims: pl.BlockSpec(dims, lambda i: (0,) * len(dims))
    operands = [full, hi, lo, twist]
    specs = [whole(128, 32, 128), whole(256, 512), whole(256, 512), whole(32, 8, 128)]
    if field is not None:
        operands.append(field)
        specs.append(pl.BlockSpec(memory_space=pl.ANY))
    return pl.pallas_call(
        functools.partial(rows_kernel, plane),
        grid=(1,),
        in_specs=specs,
        out_specs=pl.BlockSpec(memory_space=pl.ANY),
        out_shape=jax.ShapeDtypeStruct((2, 64, 8192), jnp.float32),
        scratch_shapes=[
            pltpu.VMEM((4, 32, 64, 128), jnp.float32),
            pltpu.VMEM((64, 8192), jnp.float32),
            pltpu.SemaphoreType.DMA((8,)),
        ],
        input_output_aliases={} if field is None else {4: 0},
        compiler_params=pltpu.CompilerParams(vmem_limit_bytes=VMEM_LIMIT),
        cost_estimate=pl.CostEstimate(flops=3 << 29, bytes_accessed=4 << 20, transcendentals=0),
        name="rows",
    )(*operands)


def shards(noise, root):
    lane_matrix, lane_twist = lane_tables()
    row_matrix, row_twist = row_tables()
    lane_hi, lane_lo = split_bf16(lane_matrix)
    row_hi, row_lo = split_bf16(row_matrix)
    col = lax.axis_index(COLS)[None]
    field = None
    full = []
    got = [[None] * 4 for _ in range(2)]
    for plane, partners, limit in ((0, (2,), 60 << 20), (0, (3, 1, 0), VMEM_LIMIT), (1, (2, 3, 1, 0), VMEM_LIMIT)):
        for d, piece in zip(partners, spectrum(col, noise, root, plane, partners, limit)):
            got[plane][d] = piece
    for plane in range(2):
        for d in (2, 3, 1):
            got[plane][d] = lax.ppermute(got[plane][d], COLS, [(c, c ^ d) for c in range(4)])
    for plane in range(2):
        pieces = got[plane]
        blocks = columns(col, pieces, lane_hi, lane_lo, jnp.asarray(lane_twist), 3 << (28 + 8 * plane))
        full.append(lax.all_to_all(blocks, ORDER_AXES, 0, 0, tiled=True))
    for plane in range(2):
        field = rows(full[plane], row_hi, row_lo, jnp.asarray(row_twist), plane, field)
    return field


def solution(mesh):
    split = Mesh(mesh.devices.reshape(2, 4, 4, 2, 2), ROWS + COLS)
    return jax.shard_map(
        shards,
        mesh=split,
        in_specs=(P(None, None, ROWS, COLS), P(None, ROWS, COLS)),
        out_specs=P(None, ROWS + COLS, None),
        check_vma=False,
    )
```

```python
import functools

import numpy as np
import jax
import jax.numpy as jnp
from jax import lax
from jax.experimental import pallas as pl
from jax.experimental.pallas import tpu as pltpu
from jax.sharding import Mesh, PartitionSpec as P

PITCH = 72
FIRST = 59 << 20
VMEM_LIMIT = 48 * 1024 * 1024


def split_bf16(table):
    hi = jnp.asarray(table, jnp.float32).astype(jnp.bfloat16)
    lo = (jnp.asarray(table, jnp.float32) - hi.astype(jnp.float32)).astype(jnp.bfloat16)
    return hi, lo


def unit(num, den):
    ang = 2.0 * np.pi * (np.asarray(num) % den) / den
    return np.cos(ang), np.sin(ang)


ROWS, COLS = ("y_hi", "x", "z"), ("y_lo", "core")
ORDER_AXES = ("core", "z", "x", "y_hi", "y_lo")
ORDER = np.arange(128).reshape(2, 4, 4, 2, 2).transpose(4, 2, 1, 0, 3).reshape(128)


def lane_tables():
    step = np.arange(128)
    cos, sin = unit(ORDER[:, None] * step[None, :], 128)
    matrix = np.block([[cos, -sin], [sin, cos]])
    cos, sin = unit(np.arange(64)[:, None] * step[None, :], 8192)
    twist = np.stack([cos, sin], 1).reshape(128, 128)
    return matrix, twist.astype(np.float32)


def row_tables():
    src = ORDER
    blocks = []
    for parity in (0, 1):
        cos, sin = unit(src[:, None] * (2 * np.arange(128) + parity)[None, :], 256)
        blocks.append(np.block([[cos, sin], [-sin, cos]]))
    matrix = np.concatenate(blocks, 1) / 4096.0
    twist = np.zeros((32, 8, 128))
    for parity in (0, 1):
        cos, sin = unit(np.arange(32)[:, None] * (2 * np.arange(128) + parity)[None, :], 8192)
        twist[:, 2 * parity] = cos
        twist[:, 2 * parity + 1] = sin
    return matrix, twist.astype(np.float32)


def cadd(a, b):
    return a[0] + b[0], a[1] + b[1]


def csub(a, b):
    return a[0] - b[0], a[1] - b[1]


def turn(a):
    return -a[1], a[0]


def cmul(a, cos, sin):
    return a[0] * cos - a[1] * sin, a[0] * sin + a[1] * cos


def dft4(v):
    s, d = cadd(v[0], v[2]), csub(v[0], v[2])
    t, u = cadd(v[1], v[3]), turn(csub(v[1], v[3]))
    return [cadd(s, t), cadd(d, u), csub(s, t), csub(d, u)]


HALF = float(np.sqrt(0.5))


def dft8(v):
    even, odd = dft4(v[0::2]), dft4(v[1::2])
    one = odd[1]
    one = ((one[0] - one[1]) * HALF, (one[0] + one[1]) * HALF)
    three = odd[3]
    three = ((-three[0] - three[1]) * HALF, (three[0] - three[1]) * HALF)
    odd = [odd[0], one, turn(odd[2]), three]
    return [cadd(even[i], odd[i]) for i in range(4)] + [csub(even[i], odd[i]) for i in range(4)]


def dft8_real(v):
    even, odd = dft4(v[0::2]), dft4(v[1::2])
    one, three = odd[1], odd[3]
    odd_re = [odd[0][0], (one[0] - one[1]) * HALF, -odd[2][1], (-three[0] - three[1]) * HALF]
    return [even[i][0] + odd_re[i] for i in range(4)] + [even[i][0] - odd_re[i] for i in range(4)]


def const_mul(a, num, den):
    num %= den
    if num == 0:
        return a
    if num * 4 == den:
        return turn(a)
    cos, sin = unit(num, den)
    return cmul(a, float(cos), float(sin))


def parts(x):
    hi = x.astype(jnp.bfloat16)
    return hi, (x - hi.astype(jnp.float32)).astype(jnp.bfloat16)


def spectrum_kernel(spans, partners, col_ref, noise_ref, root_ref, *rest):
    outs, (noise, root, arrived) = rest[:len(partners)], rest[len(partners):]
    copies = []
    for i, d in enumerate(partners):
        block = pl.multiple_of((col_ref[0] ^ d) * 32, 32)
        at = 0
        for j, (plane, first, count) in enumerate(spans):
            rows, here = pl.ds(pl.multiple_of(block + first, 16), count), pl.ds(at, count)
            copies += [
                pltpu.make_async_copy(noise_ref.at[0, plane, rows], noise.at[i, 0, here], arrived.at[i, j, 0]),
                pltpu.make_async_copy(noise_ref.at[1, plane, rows], noise.at[i, 1, here], arrived.at[i, j, 1]),
                pltpu.make_async_copy(root_ref.at[plane, rows], root.at[i, here], arrived.at[i, j, 2]),
            ]
            at += count
    for copy in copies:
        copy.start()
    for i, out in enumerate(outs):
        for copy in copies[3 * len(spans) * i:3 * len(spans) * (i + 1)]:
            copy.wait()
        scale = root[i].astype(jnp.float32)
        for s in (0, 1):
            out[s] = noise[i, s].astype(jnp.float32) * scale


def spectrum(col, noise, root, spans, partners, limit, first=False):
    n, count = len(partners), sum(span[2] for span in spans)
    return pl.pallas_call(
        functools.partial(spectrum_kernel, spans, partners),
        grid_spec=pltpu.PrefetchScalarGridSpec(
            num_scalar_prefetch=1,
            grid=(1,),
            in_specs=[pl.BlockSpec(memory_space=pltpu.HBM)] * 2,
            out_specs=[pl.BlockSpec((2, count, 2048), lambda i, c: (0, 0, 0))] * n,
            scratch_shapes=[
                pltpu.VMEM((n, 2, count, 2048), jnp.bfloat16),
                pltpu.VMEM((n, count, 2048), jnp.bfloat16),
                pltpu.SemaphoreType.DMA((n, len(spans), 3)),
            ],
        ),
        out_shape=[(pltpu.VMEM if first else jax.ShapeDtypeStruct)((2, count, 2048), jnp.float32)] * n,
        compiler_params=pltpu.CompilerParams(vmem_limit_bytes=limit),
        cost_estimate=pl.CostEstimate(flops=n << 18, bytes_accessed=n * (7 << 17), transcendentals=0),
        name="spectrum",
    )(col, noise, root)


def by_index(values, index):
    odd, upper = (index & 1) == 1, (index & 2) == 2
    pick = lambda flag, a, b: tuple(jnp.where(flag, p, q) for p, q in zip(a, b))
    v = [pick(odd, values[d ^ 1], values[d]) for d in range(4)]
    return [pick(upper, v[d ^ 2], v[d]) for d in range(4)]


def columns_kernel(col_ref, x0, x1, x2, x3, hi_ref, lo_ref, twist_ref, out_ref, mid, turned):
    for low in range(8):
        v = [None] * 8
        for half in range(2):
            at = (half * 8 + low) * 128
            got = [tuple(x[s, :, at:at + 128] for s in (0, 1)) for x in (x0, x1, x2, x3)]
            v[half::2] = by_index(got, col_ref[0])
        for b, value in enumerate(dft8(v)):
            value = const_mul(value, low * b, 64)
            for s in (0, 1):
                mid[s, b, low] = value[s]
    for b in range(8):
        v = [(mid[0, b, low], mid[1, b, low]) for low in range(8)]
        for h, value in enumerate(dft8(v)):
            y_low = b + 8 * h
            value = cmul(value, twist_ref[2 * y_low:2 * y_low + 1, :], twist_ref[2 * y_low + 1:2 * y_low + 2, :])
            for s in (0, 1):
                turned[s, pl.ds(y_low, 8, stride=PITCH), :] = value[s]
    flat = out_ref.reshape(128 * 8, 128)
    dims = (((1,), (1,)), ((), ()))
    for half in range(2):
        rows = [slice(k * PITCH, k * PITCH + 64) for k in range(4 * half, 4 * half + 4)]
        hi, lo = parts(jnp.concatenate([jnp.concatenate([turned[s, r, :] for r in rows], 0) for s in (0, 1)], 1))
        result = lax.dot_general(hi_ref[...], hi, dims, preferred_element_type=jnp.float32)
        result += lax.dot_general(lo_ref[...], hi, dims, preferred_element_type=jnp.float32)
        result += lax.dot_general(hi_ref[...], lo, dims, preferred_element_type=jnp.float32)
        for pair in range(2):
            for s in (0, 1):
                flat[pl.ds((half * 2 + pair) * 2 + s, 128, stride=8), :] = result[
                    s * 128:(s + 1) * 128, pair * 128:(pair + 1) * 128
                ]


def columns(col, pieces, hi, lo, twist, flops):
    return pl.pallas_call(
        columns_kernel,
        grid_spec=pltpu.PrefetchScalarGridSpec(
            num_scalar_prefetch=1,
            grid=(4,),
            in_specs=[pl.BlockSpec((2, 8, 2048), lambda i, c: (0, i, 0))] * 4
            + [
                pl.BlockSpec((256, 256), lambda i, c: (0, 0)),
                pl.BlockSpec((256, 256), lambda i, c: (0, 0)),
                pl.BlockSpec((128, 128), lambda i, c: (0, 0)),
            ],
            out_specs=pl.BlockSpec((128, 8, 128), lambda i, c: (0, i, 0)),
            scratch_shapes=[
                pltpu.VMEM((2, 8, 8, 8, 128), jnp.float32),
                pltpu.VMEM((2, 8 * PITCH, 128), jnp.float32),
            ],
        ),
        out_shape=jax.ShapeDtypeStruct((128, 32, 128), jnp.float32),
        compiler_params=pltpu.CompilerParams(vmem_limit_bytes=VMEM_LIMIT),
        cost_estimate=pl.CostEstimate(flops=flops, bytes_accessed=4 << 20, transcendentals=0),
        name="columns",
    )(col, *pieces, hi, lo, twist)


def rows_kernel(plane, c_ref, hi_ref, lo_ref, twist_ref, *rest):
    out_ref, steps, ready, sent = rest[-4:]
    flat = c_ref.reshape(128 * 32, 128)

    def some_pairs(step, _):
        both = []
        for t in range(8):
            at = 2 * (8 * step + t)
            both.append(jnp.concatenate([flat[pl.ds(at + s, 128, stride=32), :].T for s in (0, 1)], 1))
        hi, lo = parts(jnp.concatenate(both, 0))
        result = jnp.dot(hi, hi_ref[...], preferred_element_type=jnp.float32)
        result += jnp.dot(hi, lo_ref[...], preferred_element_type=jnp.float32)
        result += jnp.dot(lo, hi_ref[...], preferred_element_type=jnp.float32)
        for t in range(16):
            k = 16 * step + t
            for parity in (0, 1):
                re, im = (result[64 * t:64 * t + 64, at:at + 128] for at in (256 * parity, 256 * parity + 128))
                twist = (twist_ref[k, j:j + 1, :] for j in (2 * parity, 2 * parity + 1))
                for s, value in enumerate(cmul((re, im), *twist)):
                    steps[2 * parity + s, k] = value
        return 0

    lax.fori_loop(0, 2, some_pairs, 0)
    for s in (0, 1):
        first = flat[pl.ds(s, 128, stride=32), :].T[0:64, 0:1] * (1.0 / 4096.0)
        steps[2 - 2 * s, 0] -= first

    def copy(group):
        part = pl.ds(pl.multiple_of(group * 8, 8), 8)
        return pltpu.make_async_copy(ready.at[part], out_ref.at[plane, part], sent.at[group])

    def one_group(group, _):
        here = pl.ds(pl.multiple_of(group * 8, 8), 8)
        for parity in (0, 1):
            mid = [[None] * 8 for _ in range(4)]
            for low in range(8):
                v = [tuple(steps[2 * parity + s, 8 * high + low, here, :] for s in (0, 1)) for high in range(4)]
                for b, value in enumerate(dft4(v)):
                    mid[b][low] = const_mul(value, low * b, 32)
            for b in range(4):
                for h, value in enumerate(dft8_real(mid[b])):
                    col = (parity * 32 + b + 4 * h) * 128
                    ready[here, col:col + 128] = value
        copy(group).start()
        return 0

    lax.fori_loop(0, 8, one_group, 0, unroll=True)
    for group in range(8):
        copy(group).wait()


def rows(full, hi, lo, twist, plane, field=None):
    whole = lambda *dims: pl.BlockSpec(dims, lambda i: (0,) * len(dims))
    operands = [full, hi, lo, twist]
    specs = [whole(128, 32, 128), whole(256, 512), whole(256, 512), whole(32, 8, 128)]
    if field is not None:
        operands.append(field)
        specs.append(pl.BlockSpec(memory_space=pl.ANY))
    return pl.pallas_call(
        functools.partial(rows_kernel, plane),
        grid=(1,),
        in_specs=specs,
        out_specs=pl.BlockSpec(memory_space=pl.ANY),
        out_shape=jax.ShapeDtypeStruct((2, 64, 8192), jnp.float32),
        scratch_shapes=[
            pltpu.VMEM((4, 32, 64, 128), jnp.float32),
            pltpu.VMEM((64, 8192), jnp.float32),
            pltpu.SemaphoreType.DMA((8,)),
        ],
        input_output_aliases={} if field is None else {4: 0},
        compiler_params=pltpu.CompilerParams(vmem_limit_bytes=VMEM_LIMIT),
        cost_estimate=pl.CostEstimate(flops=3 << 29, bytes_accessed=4 << 20, transcendentals=0),
        name="rows",
    )(*operands)


def shards(noise, root):
    lane_matrix, lane_twist = lane_tables()
    row_matrix, row_twist = row_tables()
    lane_hi, lane_lo = split_bf16(lane_matrix)
    row_hi, row_lo = split_bf16(row_matrix)
    col = lax.axis_index(COLS)[None]
    field = None
    full = []
    got = [[None] * 4 for _ in range(2)]
    for plane, partners, limit in ((0, (2,), FIRST), (0, (3, 1, 0), VMEM_LIMIT), (1, (2, 3, 1, 0), VMEM_LIMIT)):
        made = spectrum(col, noise, root, ((plane, 0, 32),), partners, limit, limit == FIRST)
        for d, piece in zip(partners, made):
            got[plane][d] = piece
    for plane in range(2):
        for d in (2, 3, 1):
            got[plane][d] = lax.ppermute(got[plane][d], COLS, [(c, c ^ d) for c in range(4)])
    for plane in range(2):
        pieces = got[plane]
        blocks = columns(col, pieces, lane_hi, lane_lo, jnp.asarray(lane_twist), 3 << (28 + 8 * plane))
        full.append(lax.all_to_all(blocks, ORDER_AXES, 0, 0, tiled=True))
    for plane in range(2):
        field = rows(full[plane], row_hi, row_lo, jnp.asarray(row_twist), plane, field)
    return field


def solution(mesh):
    split = Mesh(mesh.devices.reshape(2, 4, 4, 2, 2), ROWS + COLS)
    return jax.shard_map(
        shards,
        mesh=split,
        in_specs=(P(None, None, ROWS, COLS), P(None, ROWS, COLS)),
        out_specs=P(None, ROWS + COLS, None),
        check_vma=False,
    )
```

```python
import functools

import numpy as np
import jax
import jax.numpy as jnp
from jax import lax
from jax.experimental import pallas as pl
from jax.experimental.pallas import tpu as pltpu
from jax.sharding import Mesh, PartitionSpec as P

PITCH = 72
FIRST = 59 << 20
VMEM_LIMIT = 48 * 1024 * 1024


def split_bf16(table):
    hi = jnp.asarray(table, jnp.float32).astype(jnp.bfloat16)
    lo = (jnp.asarray(table, jnp.float32) - hi.astype(jnp.float32)).astype(jnp.bfloat16)
    return hi, lo


def unit(num, den):
    ang = 2.0 * np.pi * (np.asarray(num) % den) / den
    return np.cos(ang), np.sin(ang)


ROWS, COLS = ("y_hi", "x", "z"), ("y_lo", "core")
ORDER_AXES = ("core", "z", "x", "y_hi", "y_lo")
ORDER = np.arange(128).reshape(2, 4, 4, 2, 2).transpose(4, 2, 1, 0, 3).reshape(128)


def lane_tables():
    step = np.arange(128)
    cos, sin = unit(ORDER[:, None] * step[None, :], 128)
    matrix = np.block([[cos, -sin], [sin, cos]])
    cos, sin = unit(np.arange(64)[:, None] * step[None, :], 8192)
    twist = np.stack([cos, sin], 1).reshape(128, 128)
    return matrix, twist.astype(np.float32)


def row_tables():
    src = ORDER
    blocks = []
    for parity in (0, 1):
        cos, sin = unit(src[:, None] * (2 * np.arange(128) + parity)[None, :], 256)
        blocks.append(np.block([[cos, sin], [-sin, cos]]))
    matrix = np.concatenate(blocks, 1) / 4096.0
    twist = np.zeros((32, 8, 128))
    for parity in (0, 1):
        cos, sin = unit(np.arange(32)[:, None] * (2 * np.arange(128) + parity)[None, :], 8192)
        twist[:, 2 * parity] = cos
        twist[:, 2 * parity + 1] = sin
    return matrix, twist.astype(np.float32)


def cadd(a, b):
    return a[0] + b[0], a[1] + b[1]


def csub(a, b):
    return a[0] - b[0], a[1] - b[1]


def turn(a):
    return -a[1], a[0]


def cmul(a, cos, sin):
    return a[0] * cos - a[1] * sin, a[0] * sin + a[1] * cos


def dft4(v):
    s, d = cadd(v[0], v[2]), csub(v[0], v[2])
    t, u = cadd(v[1], v[3]), turn(csub(v[1], v[3]))
    return [cadd(s, t), cadd(d, u), csub(s, t), csub(d, u)]


HALF = float(np.sqrt(0.5))


def dft8(v):
    even, odd = dft4(v[0::2]), dft4(v[1::2])
    one = odd[1]
    one = ((one[0] - one[1]) * HALF, (one[0] + one[1]) * HALF)
    three = odd[3]
    three = ((-three[0] - three[1]) * HALF, (three[0] - three[1]) * HALF)
    odd = [odd[0], one, turn(odd[2]), three]
    return [cadd(even[i], odd[i]) for i in range(4)] + [csub(even[i], odd[i]) for i in range(4)]


def dft8_real(v):
    even, odd = dft4(v[0::2]), dft4(v[1::2])
    one, three = odd[1], odd[3]
    odd_re = [odd[0][0], (one[0] - one[1]) * HALF, -odd[2][1], (-three[0] - three[1]) * HALF]
    return [even[i][0] + odd_re[i] for i in range(4)] + [even[i][0] - odd_re[i] for i in range(4)]


def const_mul(a, num, den):
    num %= den
    if num == 0:
        return a
    if num * 4 == den:
        return turn(a)
    cos, sin = unit(num, den)
    return cmul(a, float(cos), float(sin))


def parts(x):
    hi = x.astype(jnp.bfloat16)
    return hi, (x - hi.astype(jnp.float32)).astype(jnp.bfloat16)


def spectrum_kernel(spans, partners, col_ref, noise_ref, root_ref, *rest):
    outs, (noise, root, arrived) = rest[:len(partners)], rest[len(partners):]
    copies = []
    for i, d in enumerate(partners):
        block = pl.multiple_of((col_ref[0] ^ d) * 32, 32)
        at = 0
        for j, (plane, first, count) in enumerate(spans):
            rows, here = pl.ds(pl.multiple_of(block + first, 16), count), pl.ds(at, count)
            copies += [
                pltpu.make_async_copy(noise_ref.at[0, plane, rows], noise.at[i, 0, here], arrived.at[i, j, 0]),
                pltpu.make_async_copy(noise_ref.at[1, plane, rows], noise.at[i, 1, here], arrived.at[i, j, 1]),
                pltpu.make_async_copy(root_ref.at[plane, rows], root.at[i, here], arrived.at[i, j, 2]),
            ]
            at += count
    for copy in copies:
        copy.start()
    for i, out in enumerate(outs):
        for copy in copies[3 * len(spans) * i:3 * len(spans) * (i + 1)]:
            copy.wait()
        scale = root[i].astype(jnp.float32)
        for s in (0, 1):
            out[s] = noise[i, s].astype(jnp.float32) * scale


def spectrum(col, noise, root, spans, partners, limit, first=False):
    n, count = len(partners), sum(span[2] for span in spans)
    return pl.pallas_call(
        functools.partial(spectrum_kernel, spans, partners),
        grid_spec=pltpu.PrefetchScalarGridSpec(
            num_scalar_prefetch=1,
            grid=(1,),
            in_specs=[pl.BlockSpec(memory_space=pltpu.HBM)] * 2,
            out_specs=[pl.BlockSpec((2, count, 2048), lambda i, c: (0, 0, 0))] * n,
            scratch_shapes=[
                pltpu.VMEM((n, 2, count, 2048), jnp.bfloat16),
                pltpu.VMEM((n, count, 2048), jnp.bfloat16),
                pltpu.SemaphoreType.DMA((n, len(spans), 3)),
            ],
        ),
        out_shape=[(pltpu.VMEM if first else jax.ShapeDtypeStruct)((2, count, 2048), jnp.float32)] * n,
        compiler_params=pltpu.CompilerParams(vmem_limit_bytes=limit),
        cost_estimate=pl.CostEstimate(flops=n << 18, bytes_accessed=n * (7 << 17), transcendentals=0),
        name="spectrum",
    )(col, noise, root)


def by_index(values, index):
    odd, upper = (index & 1) == 1, (index & 2) == 2
    pick = lambda flag, a, b: tuple(jnp.where(flag, p, q) for p, q in zip(a, b))
    v = [pick(odd, values[d ^ 1], values[d]) for d in range(4)]
    return [pick(upper, v[d ^ 2], v[d]) for d in range(4)]


def columns_kernel(col_ref, x0, x1, x2, x3, hi_ref, lo_ref, twist_ref, out_ref, mid, turned):
    for low in range(8):
        v = [None] * 8
        for half in range(2):
            at = (half * 8 + low) * 128
            got = [tuple(x[s, :, at:at + 128] for s in (0, 1)) for x in (x0, x1, x2, x3)]
            v[half::2] = by_index(got, col_ref[0])
        for b, value in enumerate(dft8(v)):
            value = const_mul(value, low * b, 64)
            for s in (0, 1):
                mid[s, b, low] = value[s]
    for b in range(8):
        v = [(mid[0, b, low], mid[1, b, low]) for low in range(8)]
        for h, value in enumerate(dft8(v)):
            y_low = b + 8 * h
            value = cmul(value, twist_ref[2 * y_low:2 * y_low + 1, :], twist_ref[2 * y_low + 1:2 * y_low + 2, :])
            for s in (0, 1):
                turned[s, pl.ds(y_low, 8, stride=PITCH), :] = value[s]
    flat = out_ref.reshape(128 * 8, 128)
    dims = (((1,), (1,)), ((), ()))
    for half in range(2):
        rows = [slice(k * PITCH, k * PITCH + 64) for k in range(4 * half, 4 * half + 4)]
        hi, lo = parts(jnp.concatenate([jnp.concatenate([turned[s, r, :] for r in rows], 0) for s in (0, 1)], 1))
        result = lax.dot_general(hi_ref[...], hi, dims, preferred_element_type=jnp.float32)
        result += lax.dot_general(lo_ref[...], hi, dims, preferred_element_type=jnp.float32)
        result += lax.dot_general(hi_ref[...], lo, dims, preferred_element_type=jnp.float32)
        for pair in range(2):
            for s in (0, 1):
                flat[pl.ds((half * 2 + pair) * 2 + s, 128, stride=8), :] = result[
                    s * 128:(s + 1) * 128, pair * 128:(pair + 1) * 128
                ]


def columns(col, pieces, hi, lo, twist, flops):
    return pl.pallas_call(
        columns_kernel,
        grid_spec=pltpu.PrefetchScalarGridSpec(
            num_scalar_prefetch=1,
            grid=(4,),
            in_specs=[pl.BlockSpec((2, 8, 2048), lambda i, c: (0, i, 0))] * 4
            + [
                pl.BlockSpec((256, 256), lambda i, c: (0, 0)),
                pl.BlockSpec((256, 256), lambda i, c: (0, 0)),
                pl.BlockSpec((128, 128), lambda i, c: (0, 0)),
            ],
            out_specs=pl.BlockSpec((128, 8, 128), lambda i, c: (0, i, 0)),
            scratch_shapes=[
                pltpu.VMEM((2, 8, 8, 8, 128), jnp.float32),
                pltpu.VMEM((2, 8 * PITCH, 128), jnp.float32),
            ],
        ),
        out_shape=jax.ShapeDtypeStruct((128, 32, 128), jnp.float32),
        compiler_params=pltpu.CompilerParams(vmem_limit_bytes=VMEM_LIMIT),
        cost_estimate=pl.CostEstimate(flops=flops, bytes_accessed=4 << 20, transcendentals=0),
        name="columns",
    )(col, *pieces, hi, lo, twist)


def rows_kernel(plane, c_ref, hi_ref, lo_ref, twist_ref, *rest):
    out_ref, steps, ready, sent = rest[-4:]
    flat = c_ref.reshape(128 * 32, 128)

    def some_pairs(step):
        both = []
        for t in range(8):
            at = 2 * (8 * step + t)
            both.append(jnp.concatenate([flat[pl.ds(at + s, 128, stride=32), :].T for s in (0, 1)], 1))
        hi, lo = parts(jnp.concatenate(both, 0))
        result = jnp.dot(hi, hi_ref[...], preferred_element_type=jnp.float32)
        result += jnp.dot(hi, lo_ref[...], preferred_element_type=jnp.float32)
        result += jnp.dot(lo, hi_ref[...], preferred_element_type=jnp.float32)
        for t in range(16):
            k = 16 * step + t
            for parity in (0, 1):
                re, im = (result[64 * t:64 * t + 64, at:at + 128] for at in (256 * parity, 256 * parity + 128))
                twist = (twist_ref[k, j:j + 1, :] for j in (2 * parity, 2 * parity + 1))
                for s, value in enumerate(cmul((re, im), *twist)):
                    steps[2 * parity + s, k] = value

    for step in range(2):
        some_pairs(step)
    for s in (0, 1):
        first = flat[pl.ds(s, 128, stride=32), :].T[0:64, 0:1] * (1.0 / 4096.0)
        steps[2 - 2 * s, 0] -= first

    def copy(group):
        part = pl.ds(group * 8, 8)
        return pltpu.make_async_copy(ready.at[part], out_ref.at[plane, part], sent.at[group])

    def one_group(group):
        here = pl.ds(group * 8, 8)
        for parity in (0, 1):
            mid = [[None] * 8 for _ in range(4)]
            for low in range(8):
                v = [tuple(steps[2 * parity + s, 8 * high + low, here, :] for s in (0, 1)) for high in range(4)]
                for b, value in enumerate(dft4(v)):
                    mid[b][low] = const_mul(value, low * b, 32)
            for b in range(4):
                for h, value in enumerate(dft8_real(mid[b])):
                    col = (parity * 32 + b + 4 * h) * 128
                    ready[here, col:col + 128] = value
        copy(group).start()

    for group in range(8):
        one_group(group)
    for group in range(8):
        copy(group).wait()


def rows(full, hi, lo, twist, plane, field=None):
    whole = lambda *dims: pl.BlockSpec(dims, lambda i: (0,) * len(dims))
    operands = [full, hi, lo, twist]
    specs = [whole(128, 32, 128), whole(256, 512), whole(256, 512), whole(32, 8, 128)]
    if field is not None:
        operands.append(field)
        specs.append(pl.BlockSpec(memory_space=pl.ANY))
    return pl.pallas_call(
        functools.partial(rows_kernel, plane),
        grid=(1,),
        in_specs=specs,
        out_specs=pl.BlockSpec(memory_space=pl.ANY),
        out_shape=jax.ShapeDtypeStruct((2, 64, 8192), jnp.float32),
        scratch_shapes=[
            pltpu.VMEM((4, 32, 64, 128), jnp.float32),
            pltpu.VMEM((64, 8192), jnp.float32),
            pltpu.SemaphoreType.DMA((8,)),
        ],
        input_output_aliases={} if field is None else {4: 0},
        compiler_params=pltpu.CompilerParams(vmem_limit_bytes=VMEM_LIMIT),
        cost_estimate=pl.CostEstimate(flops=3 << 29, bytes_accessed=4 << 20, transcendentals=0),
        name="rows",
    )(*operands)


def shards(noise, root):
    lane_matrix, lane_twist = lane_tables()
    row_matrix, row_twist = row_tables()
    lane_hi, lane_lo = split_bf16(lane_matrix)
    row_hi, row_lo = split_bf16(row_matrix)
    col = lax.axis_index(COLS)[None]
    field = None
    full = []
    got = [[None] * 4 for _ in range(2)]
    for plane, partners, limit in ((0, (2,), FIRST), (0, (3, 1, 0), VMEM_LIMIT), (1, (2, 3, 1, 0), VMEM_LIMIT)):
        made = spectrum(col, noise, root, ((plane, 0, 32),), partners, limit, limit == FIRST)
        for d, piece in zip(partners, made):
            got[plane][d] = piece
    for plane in range(2):
        for d in (2, 3, 1):
            got[plane][d] = lax.ppermute(got[plane][d], COLS, [(c, c ^ d) for c in range(4)])
    for plane in range(2):
        pieces = got[plane]
        blocks = columns(col, pieces, lane_hi, lane_lo, jnp.asarray(lane_twist), 3 << (28 + 8 * plane))
        full.append(lax.all_to_all(blocks, ORDER_AXES, 0, 0, tiled=True))
    for plane in range(2):
        field = rows(full[plane], row_hi, row_lo, jnp.asarray(row_twist), plane, field)
    return field


def solution(mesh):
    split = Mesh(mesh.devices.reshape(2, 4, 4, 2, 2), ROWS + COLS)
    return jax.shard_map(
        shards,
        mesh=split,
        in_specs=(P(None, None, ROWS, COLS), P(None, ROWS, COLS)),
        out_specs=P(None, ROWS + COLS, None),
        check_vma=False,
    )
```

```python
import functools

import numpy as np
import jax
import jax.numpy as jnp
from jax import lax
from jax.experimental import pallas as pl
from jax.experimental.pallas import tpu as pltpu
from jax.sharding import Mesh, PartitionSpec as P

PITCH = 72
FIRST = 59 << 20
VMEM_LIMIT = 48 * 1024 * 1024


def split_bf16(table):
    hi = jnp.asarray(table, jnp.float32).astype(jnp.bfloat16)
    lo = (jnp.asarray(table, jnp.float32) - hi.astype(jnp.float32)).astype(jnp.bfloat16)
    return hi, lo


def unit(num, den):
    ang = 2.0 * np.pi * (np.asarray(num) % den) / den
    return np.cos(ang), np.sin(ang)


ROWS, COLS = ("y_hi", "x", "z"), ("y_lo", "core")
ORDER_AXES = ("core", "z", "x", "y_lo", "y_hi")
ORDER = np.arange(128).reshape(2, 4, 4, 2, 2).transpose(4, 2, 1, 3, 0).reshape(128)


def lane_tables():
    step = np.arange(128)
    cos, sin = unit(ORDER[:, None] * step[None, :], 128)
    matrix = np.block([[cos, -sin], [sin, cos]])
    cos, sin = unit(np.arange(64)[:, None] * step[None, :], 8192)
    twist = np.stack([cos, sin], 1).reshape(128, 128)
    return matrix, twist.astype(np.float32)


def row_tables():
    src = ORDER
    blocks = []
    for parity in (0, 1):
        cos, sin = unit(src[:, None] * (2 * np.arange(128) + parity)[None, :], 256)
        blocks.append(np.block([[cos, sin], [-sin, cos]]))
    matrix = np.concatenate(blocks, 1) / 4096.0
    twist = np.zeros((32, 8, 128))
    for parity in (0, 1):
        cos, sin = unit(np.arange(32)[:, None] * (2 * np.arange(128) + parity)[None, :], 8192)
        twist[:, 2 * parity] = cos
        twist[:, 2 * parity + 1] = sin
    return matrix, twist.astype(np.float32)


def cadd(a, b):
    return a[0] + b[0], a[1] + b[1]


def csub(a, b):
    return a[0] - b[0], a[1] - b[1]


def turn(a):
    return -a[1], a[0]


def cmul(a, cos, sin):
    return a[0] * cos - a[1] * sin, a[0] * sin + a[1] * cos


def dft4(v):
    s, d = cadd(v[0], v[2]), csub(v[0], v[2])
    t, u = cadd(v[1], v[3]), turn(csub(v[1], v[3]))
    return [cadd(s, t), cadd(d, u), csub(s, t), csub(d, u)]


HALF = float(np.sqrt(0.5))


def dft8(v):
    even, odd = dft4(v[0::2]), dft4(v[1::2])
    one = odd[1]
    one = ((one[0] - one[1]) * HALF, (one[0] + one[1]) * HALF)
    three = odd[3]
    three = ((-three[0] - three[1]) * HALF, (three[0] - three[1]) * HALF)
    odd = [odd[0], one, turn(odd[2]), three]
    return [cadd(even[i], odd[i]) for i in range(4)] + [csub(even[i], odd[i]) for i in range(4)]


def dft8_real(v):
    even, odd = dft4(v[0::2]), dft4(v[1::2])
    one, three = odd[1], odd[3]
    odd_re = [odd[0][0], (one[0] - one[1]) * HALF, -odd[2][1], (-three[0] - three[1]) * HALF]
    return [even[i][0] + odd_re[i] for i in range(4)] + [even[i][0] - odd_re[i] for i in range(4)]


def const_mul(a, num, den):
    num %= den
    if num == 0:
        return a
    if num * 4 == den:
        return turn(a)
    cos, sin = unit(num, den)
    return cmul(a, float(cos), float(sin))


def parts(x):
    hi = x.astype(jnp.bfloat16)
    return hi, (x - hi.astype(jnp.float32)).astype(jnp.bfloat16)


def spectrum_kernel(spans, partners, col_ref, noise_ref, root_ref, *rest):
    outs, (noise, root, arrived) = rest[:len(partners)], rest[len(partners):]
    copies = []
    for i, d in enumerate(partners):
        block = pl.multiple_of((col_ref[0] ^ d) * 32, 32)
        at = 0
        for j, (plane, first, count) in enumerate(spans):
            rows, here = pl.ds(pl.multiple_of(block + first, 16), count), pl.ds(at, count)
            copies += [
                pltpu.make_async_copy(noise_ref.at[0, plane, rows], noise.at[i, 0, here], arrived.at[i, j, 0]),
                pltpu.make_async_copy(noise_ref.at[1, plane, rows], noise.at[i, 1, here], arrived.at[i, j, 1]),
                pltpu.make_async_copy(root_ref.at[plane, rows], root.at[i, here], arrived.at[i, j, 2]),
            ]
            at += count
    for copy in copies:
        copy.start()
    for i, out in enumerate(outs):
        for copy in copies[3 * len(spans) * i:3 * len(spans) * (i + 1)]:
            copy.wait()
        scale = root[i].astype(jnp.float32)
        for s in (0, 1):
            out[s] = noise[i, s].astype(jnp.float32) * scale


def spectrum(col, noise, root, spans, partners, limit, first=False):
    n, count = len(partners), sum(span[2] for span in spans)
    return pl.pallas_call(
        functools.partial(spectrum_kernel, spans, partners),
        grid_spec=pltpu.PrefetchScalarGridSpec(
            num_scalar_prefetch=1,
            grid=(1,),
            in_specs=[pl.BlockSpec(memory_space=pltpu.HBM)] * 2,
            out_specs=[pl.BlockSpec((2, count, 2048), lambda i, c: (0, 0, 0))] * n,
            scratch_shapes=[
                pltpu.VMEM((n, 2, count, 2048), jnp.bfloat16),
                pltpu.VMEM((n, count, 2048), jnp.bfloat16),
                pltpu.SemaphoreType.DMA((n, len(spans), 3)),
            ],
        ),
        out_shape=[(pltpu.VMEM if first else jax.ShapeDtypeStruct)((2, count, 2048), jnp.float32)] * n,
        compiler_params=pltpu.CompilerParams(vmem_limit_bytes=limit),
        cost_estimate=pl.CostEstimate(flops=n << 18, bytes_accessed=n * (7 << 17), transcendentals=0),
        name="spectrum",
    )(col, noise, root)


def by_index(values, index):
    odd, upper = (index & 1) == 1, (index & 2) == 2
    pick = lambda flag, a, b: tuple(jnp.where(flag, p, q) for p, q in zip(a, b))
    v = [pick(odd, values[d ^ 1], values[d]) for d in range(4)]
    return [pick(upper, v[d ^ 2], v[d]) for d in range(4)]


def columns_kernel(col_ref, x0, x1, x2, x3, hi_ref, lo_ref, twist_ref, out_ref, mid, turned):
    for low in range(8):
        v = [None] * 8
        for half in range(2):
            at = (half * 8 + low) * 128
            got = [tuple(x[s, :, at:at + 128] for s in (0, 1)) for x in (x0, x1, x2, x3)]
            v[half::2] = by_index(got, col_ref[0])
        for b, value in enumerate(dft8(v)):
            value = const_mul(value, low * b, 64)
            for s in (0, 1):
                mid[s, b, low] = value[s]
    for b in range(8):
        v = [(mid[0, b, low], mid[1, b, low]) for low in range(8)]
        for h, value in enumerate(dft8(v)):
            y_low = b + 8 * h
            value = cmul(value, twist_ref[2 * y_low:2 * y_low + 1, :], twist_ref[2 * y_low + 1:2 * y_low + 2, :])
            for s in (0, 1):
                turned[s, pl.ds(y_low, 8, stride=PITCH), :] = value[s]
    flat = out_ref.reshape(128 * 8, 128)
    dims = (((1,), (1,)), ((), ()))
    for half in range(2):
        rows = [slice(k * PITCH, k * PITCH + 64) for k in range(4 * half, 4 * half + 4)]
        hi, lo = parts(jnp.concatenate([jnp.concatenate([turned[s, r, :] for r in rows], 0) for s in (0, 1)], 1))
        result = lax.dot_general(hi_ref[...], hi, dims, preferred_element_type=jnp.float32)
        result += lax.dot_general(lo_ref[...], hi, dims, preferred_element_type=jnp.float32)
        result += lax.dot_general(hi_ref[...], lo, dims, preferred_element_type=jnp.float32)
        for pair in range(2):
            for s in (0, 1):
                flat[pl.ds((half * 2 + pair) * 2 + s, 128, stride=8), :] = result[
                    s * 128:(s + 1) * 128, pair * 128:(pair + 1) * 128
                ]


def columns(col, pieces, hi, lo, twist, flops):
    return pl.pallas_call(
        columns_kernel,
        grid_spec=pltpu.PrefetchScalarGridSpec(
            num_scalar_prefetch=1,
            grid=(4,),
            in_specs=[pl.BlockSpec((2, 8, 2048), lambda i, c: (0, i, 0))] * 4
            + [
                pl.BlockSpec((256, 256), lambda i, c: (0, 0)),
                pl.BlockSpec((256, 256), lambda i, c: (0, 0)),
                pl.BlockSpec((128, 128), lambda i, c: (0, 0)),
            ],
            out_specs=pl.BlockSpec((128, 8, 128), lambda i, c: (0, i, 0)),
            scratch_shapes=[
                pltpu.VMEM((2, 8, 8, 8, 128), jnp.float32),
                pltpu.VMEM((2, 8 * PITCH, 128), jnp.float32),
            ],
        ),
        out_shape=jax.ShapeDtypeStruct((128, 32, 128), jnp.float32),
        compiler_params=pltpu.CompilerParams(vmem_limit_bytes=VMEM_LIMIT),
        cost_estimate=pl.CostEstimate(flops=flops, bytes_accessed=4 << 20, transcendentals=0),
        name="columns",
    )(col, *pieces, hi, lo, twist)


def rows_kernel(plane, c_ref, hi_ref, lo_ref, twist_ref, *rest):
    out_ref, steps, ready, sent = rest[-4:]
    flat = c_ref.reshape(128 * 32, 128)

    def some_pairs(step):
        both = []
        for t in range(8):
            at = 2 * (8 * step + t)
            both.append(jnp.concatenate([flat[pl.ds(at + s, 128, stride=32), :].T for s in (0, 1)], 1))
        hi, lo = parts(jnp.concatenate(both, 0))
        result = jnp.dot(hi, hi_ref[...], preferred_element_type=jnp.float32)
        result += jnp.dot(hi, lo_ref[...], preferred_element_type=jnp.float32)
        result += jnp.dot(lo, hi_ref[...], preferred_element_type=jnp.float32)
        for t in range(16):
            k = 16 * step + t
            for parity in (0, 1):
                re, im = (result[64 * t:64 * t + 64, at:at + 128] for at in (256 * parity, 256 * parity + 128))
                twist = (twist_ref[k, j:j + 1, :] for j in (2 * parity, 2 * parity + 1))
                for s, value in enumerate(cmul((re, im), *twist)):
                    steps[2 * parity + s, k] = value

    for step in range(2):
        some_pairs(step)
    for s in (0, 1):
        first = flat[pl.ds(s, 128, stride=32), :].T[0:64, 0:1] * (1.0 / 4096.0)
        steps[2 - 2 * s, 0] -= first

    def copy(group):
        part = pl.ds(group * 8, 8)
        return pltpu.make_async_copy(ready.at[part], out_ref.at[plane, part], sent.at[group])

    def one_group(group):
        here = pl.ds(group * 8, 8)
        for parity in (0, 1):
            mid = [[None] * 8 for _ in range(4)]
            for low in range(8):
                v = [tuple(steps[2 * parity + s, 8 * high + low, here, :] for s in (0, 1)) for high in range(4)]
                for b, value in enumerate(dft4(v)):
                    mid[b][low] = const_mul(value, low * b, 32)
            for b in range(4):
                for h, value in enumerate(dft8_real(mid[b])):
                    col = (parity * 32 + b + 4 * h) * 128
                    ready[here, col:col + 128] = value
        copy(group).start()

    for group in range(8):
        one_group(group)
    for group in range(8):
        copy(group).wait()


def rows(full, hi, lo, twist, plane, field=None):
    whole = lambda *dims: pl.BlockSpec(dims, lambda i: (0,) * len(dims))
    operands = [full, hi, lo, twist]
    specs = [whole(128, 32, 128), whole(256, 512), whole(256, 512), whole(32, 8, 128)]
    if field is not None:
        operands.append(field)
        specs.append(pl.BlockSpec(memory_space=pl.ANY))
    return pl.pallas_call(
        functools.partial(rows_kernel, plane),
        grid=(1,),
        in_specs=specs,
        out_specs=pl.BlockSpec(memory_space=pl.ANY),
        out_shape=jax.ShapeDtypeStruct((2, 64, 8192), jnp.float32),
        scratch_shapes=[
            pltpu.VMEM((4, 32, 64, 128), jnp.float32),
            pltpu.VMEM((64, 8192), jnp.float32),
            pltpu.SemaphoreType.DMA((8,)),
        ],
        input_output_aliases={} if field is None else {4: 0},
        compiler_params=pltpu.CompilerParams(vmem_limit_bytes=VMEM_LIMIT),
        cost_estimate=pl.CostEstimate(flops=3 << 29, bytes_accessed=4 << 20, transcendentals=0),
        name="rows",
    )(*operands)


def shards(noise, root):
    lane_matrix, lane_twist = lane_tables()
    row_matrix, row_twist = row_tables()
    lane_hi, lane_lo = split_bf16(lane_matrix)
    row_hi, row_lo = split_bf16(row_matrix)
    col = lax.axis_index(COLS)[None]
    field = None
    full = []
    got = [[None] * 4 for _ in range(2)]
    for plane, partners, limit in ((0, (2,), FIRST), (0, (3, 1, 0), VMEM_LIMIT), (1, (2, 3, 1, 0), VMEM_LIMIT)):
        made = spectrum(col, noise, root, ((plane, 0, 32),), partners, limit, limit == FIRST)
        for d, piece in zip(partners, made):
            got[plane][d] = piece
    for plane in range(2):
        for d in (2, 3, 1):
            got[plane][d] = lax.ppermute(got[plane][d], COLS, [(c, c ^ d) for c in range(4)])
    for plane in range(2):
        pieces = got[plane]
        blocks = columns(col, pieces, lane_hi, lane_lo, jnp.asarray(lane_twist), 3 << (28 + 8 * plane))
        full.append(lax.all_to_all(blocks, ORDER_AXES, 0, 0, tiled=True))
    for plane in range(2):
        field = rows(full[plane], row_hi, row_lo, jnp.asarray(row_twist), plane, field)
    return field


def solution(mesh):
    split = Mesh(mesh.devices.reshape(2, 4, 4, 2, 2), ROWS + COLS)
    return jax.shard_map(
        shards,
        mesh=split,
        in_specs=(P(None, None, ROWS, COLS), P(None, ROWS, COLS)),
        out_specs=P(None, ROWS + COLS, None),
        check_vma=False,
    )
```
